32 devices in a mesh: tok: 2 (over x), dict: 16 (over z, y, core).
Axes of the slice: x: 2, y: 2, z: 4, core: 2. Of those that a mesh axis runs over, the one named last changes fastest.
Arguments:
- inputs: bfloat16 [1024, 4608], P('tok', 'dict'), may hold values from -6 to 6
- target: bfloat16 [1024, 4608], P('tok', 'dict'), may hold values from -6 to 6
- enc_weight: bfloat16 [4608, 2048], P(None, 'dict'), may hold values from -0.09375 to 0.09375
- enc_bias: float32 [2048], P('dict'), may hold values from -3 to 3
- dec_weight: bfloat16 [2048, 4608], P('dict'), may hold values from -0.75 to 0.75
- dec_bias: float32 [4608], P('dict'), may hold values from -3 to 3
- skip_weight: bfloat16 [4608, 4608], P(None, 'dict'), may hold values from -0.09375 to 0.09375
- block_ids: int32 [1024, 4], P('tok'), may hold values from 0 to 127, as said below
- slot_lists: int32 [2, 16, 384], P('tok'), may hold values from 0 to 2047, as said below
- slot_counts: int32 [2, 16], P('tok'), may hold values from 0 to 384, as said below
Outputs:
- grad_enc: float32 [4608, 2048], P('tok', 'dict')
- grad_dec: float32 [2048, 4608], P('dict', 'tok')
- grad_skip: float32 [4608, 4608], P('tok', 'dict')
The draws below stay inside these ranges and needn't reach their ends.
Inputs may be any that keep to these rules, and one draw needn't show every extreme that they name: `block_ids`: each token names 4 different blocks of 16 latents. `slot_lists`: A valid slot of list (g, o) holds a code index t * 4 + r of group g (its token t, the token's r-th block); every code of a group stands in exactly one valid slot, in the list of the owner of its block; invalid slots hold 0. `slot_counts`: in every group some list is full.
All inputs are finite; a program needn't handle non-finite values.
Results may differ from the reference program's by a relative error of at most 0.012.
Values may be sent and summed in bfloat16 or wider, within the bound.
A program may use at most 64 MiB of HBM per device.

```python
import math
import jax
import jax.numpy as jnp
from jax import lax

D = 4608
LAT_DEV = 128
BLK = 16
TOPB = 4
TOK = 512
GROUPS = 2
TOKENS = 1024
LATENTS = 2048
BPO = 8
MEAN = 128
CAP = 384
N_TOK = 2
N_DICT = 16


def group_plan(key):
    key_order, key_items, key_spread, key_base = jax.random.split(key, 4)
    order = jax.random.permutation(key_order, N_DICT).astype(jnp.int32)
    spread = jax.random.randint(key_spread, ((N_DICT - 4) // 2,), 0, MEAN + 1).astype(jnp.int32)
    paired = jnp.stack([MEAN + spread, MEAN - spread], axis=1).reshape(-1)
    head = jnp.array([CAP, 0, 0, MEAN], dtype=jnp.int32)
    by_position = jnp.concatenate([head, paired]).astype(jnp.int32)
    counts = jnp.zeros((N_DICT,), jnp.int32).at[order].set(by_position)
    ends = jnp.cumsum(counts).astype(jnp.int32)
    starts = ends - counts
    items = jax.random.permutation(key_items, TOK * TOPB).astype(jnp.int32)
    slot = jnp.arange(CAP, dtype=jnp.int32)
    place = jnp.clip(starts[:, None] + slot[None, :], 0, TOK * TOPB - 1)
    valid = slot[None, :] < counts[:, None]
    lists = jnp.where(valid, items[place], 0).astype(jnp.int32)
    position = jnp.arange(TOK * TOPB, dtype=jnp.int32)
    owner_at = jnp.sum((position[:, None] >= ends[None, :]).astype(jnp.int32), axis=1)
    owner_of_item = jnp.zeros((TOK * TOPB,), jnp.int32).at[items].set(owner_at)
    base = jax.random.randint(key_base, (TOK, 1), 0, BPO).astype(jnp.int32)
    rounds = jnp.arange(TOPB, dtype=jnp.int32)[None, :]
    local = (base + rounds) % BPO
    blocks = owner_of_item.reshape(TOK, TOPB) * BPO + local
    return (blocks.astype(jnp.int32), lists, counts)


def all_groups(key):
    keys = jax.random.split(jax.random.fold_in(key, 11), GROUPS)
    return jax.vmap(group_plan)(keys)


def draw_block_ids(key, part):
    blocks, lists, counts = all_groups(key)
    return blocks.reshape(TOKENS, TOPB)


def draw_slot_lists(key, part):
    blocks, lists, counts = all_groups(key)
    return lists


def draw_slot_counts(key, part):
    blocks, lists, counts = all_groups(key)
    return counts


def levels(own_key, shape, cuts, smallest, largest):
    loudness, own = 1.0, jax.random.fold_in(own_key, 6)
    for axis_at, shards_of in cuts:
        draws = jnp.exp(jax.random.uniform(jax.random.fold_in(own, axis_at), (shards_of,), jnp.float32, smallest / len(cuts), largest / len(cuts)))
        loudness = loudness * jnp.repeat(draws, shape[axis_at] // shards_of).reshape([-1 if axis == axis_at else 1 for axis in range(len(shape))])
    return loudness


def bell_draw(stream_key, shape, scale, most, cuts=(), kind=jnp.bfloat16):
    values = scale * jax.random.normal(stream_key, shape, jnp.float32)
    if cuts:
        values = values * levels(stream_key, shape, cuts, -0.22, 0.18)
    return jnp.clip(values, -most, most).astype(kind)


def setup_inputs(seed: int = 0) -> dict:
    seeds = jax.random.split(jax.random.key(seed), 11)
    return {
        "inputs": bell_draw(seeds[0], (TOKENS, D), 1.0, 6.0, ((0, 2), (1, 16))),
        "target": bell_draw(seeds[1], (TOKENS, D), 1.0, 6.0, ((0, 2), (1, 16))),
        "enc_weight": bell_draw(seeds[2], (D, LATENTS), D ** -0.5, 0.09375, ((1, 16),)),
        "enc_bias": bell_draw(seeds[3], (LATENTS,), 0.5, 3.0, ((0, 16),), jnp.float32),
        "dec_weight": bell_draw(seeds[4], (LATENTS, D), (BLK * TOPB) ** -0.5, 0.75, ((0, 16),)),
        "dec_bias": bell_draw(seeds[5], (D,), 0.5, 3.0, ((0, 16),), jnp.float32),
        "skip_weight": bell_draw(seeds[6], (D, D), D ** -0.5, 0.09375, ((1, 16),)),
        "block_ids": draw_block_ids(jax.random.fold_in(seeds[10], 71), 0),
        "slot_lists": draw_slot_lists(jax.random.fold_in(seeds[10], 71), 0),
        "slot_counts": draw_slot_counts(jax.random.fold_in(seeds[10], 71), 0),
    }


def gelu_pair(pre):
    factor = math.sqrt(2.0 / math.pi)
    inner = jnp.tanh(factor * (pre + 0.044715 * pre * pre * pre))
    value = 0.5 * pre * (1.0 + inner)
    slope = 0.5 * (1.0 + inner) + 0.5 * pre * (1.0 - inner * inner) * factor * (1.0 + 3.0 * 0.044715 * pre * pre)
    return (value, slope)

def owner_codes(x_group, blocks_flat, slots, count, owner, enc_part, bias_part):
    rows = slots // TOPB
    blocks = blocks_flat[slots]
    latent = owner * LAT_DEV + jnp.arange(LAT_DEV, dtype=jnp.int32)
    valid = jnp.arange(CAP, dtype=jnp.int32) < count
    active = (latent[None, :] // BLK == blocks[:, None]) & valid[:, None]
    picked = x_group[rows]
    pre = jnp.dot(picked, enc_part, preferred_element_type=jnp.float32) + bias_part[None, :]
    value, slope = gelu_pair(pre)
    code = jnp.where(active, value, 0.0).astype(jnp.bfloat16)
    return (rows, active, picked, code, slope)

def reference(inputs, target, enc_weight, enc_bias, dec_weight, dec_bias, skip_weight, block_ids, slot_lists, slot_counts):
    scale = 1.0 / math.sqrt(TOKENS)
    enc_parts = enc_weight.reshape(D, N_DICT, LAT_DEV).transpose(1, 0, 2)
    bias_parts = enc_bias.reshape(N_DICT, LAT_DEV)
    dec_parts = dec_weight.reshape(N_DICT, LAT_DEV, D)
    owners = jnp.arange(N_DICT, dtype=jnp.int32)

    def group_step(carry, group):
        start = (group * TOK).astype(jnp.int32)
        x_group = lax.dynamic_slice_in_dim(inputs, start, TOK, 0)
        y_group = lax.dynamic_slice_in_dim(target, start, TOK, 0)
        blocks_flat = lax.dynamic_slice_in_dim(block_ids, start, TOK, 0).reshape(-1)
        slots_group = slot_lists[group]
        counts_group = slot_counts[group]

        def forward_one(owner):
            rows, active, picked, code, slope = owner_codes(x_group, blocks_flat, slots_group[owner], counts_group[owner], owner, enc_parts[owner], bias_parts[owner])
            return jnp.dot(code, dec_parts[owner], preferred_element_type=jnp.float32).astype(jnp.bfloat16)
        decoded = lax.map(forward_one, owners).reshape(N_DICT * CAP, D)
        rows_all = (slots_group // TOPB).reshape(-1)
        valid_all = (jnp.arange(CAP, dtype=jnp.int32)[None, :] < counts_group[:, None]).reshape(-1)
        placed = jnp.where(valid_all[:, None], decoded.astype(jnp.float32), 0.0)
        recon = jnp.zeros((TOK, D), jnp.float32).at[rows_all].add(placed)
        skip = jnp.dot(x_group, skip_weight, preferred_element_type=jnp.float32)
        err = recon + skip + dec_bias[None, :] - y_group.astype(jnp.float32)
        grad_out = (err * scale).astype(jnp.bfloat16)

        def backward_one(owner):
            rows, active, picked, code, slope = owner_codes(x_group, blocks_flat, slots_group[owner], counts_group[owner], owner, enc_parts[owner], bias_parts[owner])
            grad_rows = grad_out[rows]
            back = jnp.dot(grad_rows, dec_parts[owner].T, preferred_element_type=jnp.float32)
            dpre = jnp.where(active, back * slope, 0.0).astype(jnp.bfloat16)
            enc_term = jnp.dot(picked.T, dpre, preferred_element_type=jnp.float32).astype(jnp.bfloat16)
            dec_term = jnp.dot(code.T, grad_rows, preferred_element_type=jnp.float32).astype(jnp.bfloat16)
            return (enc_term, dec_term)
        enc_terms, dec_terms = lax.map(backward_one, owners)
        skip_term = jnp.dot(x_group.T, grad_out, preferred_element_type=jnp.float32).astype(jnp.bfloat16)
        enc_total, dec_total, skip_total = carry
        return ((enc_total + enc_terms.astype(jnp.float32), dec_total + dec_terms.astype(jnp.float32), skip_total + skip_term.astype(jnp.float32)), None)
    start_carry = (jnp.zeros((N_DICT, D, LAT_DEV), jnp.float32), jnp.zeros((N_DICT, LAT_DEV, D), jnp.float32), jnp.zeros((D, D), jnp.float32))
    totals, unused = lax.scan(group_step, start_carry, jnp.arange(N_TOK, dtype=jnp.int32))
    enc_total, dec_total, skip_total = totals
    grad_enc = enc_total.transpose(1, 0, 2).reshape(D, LATENTS)
    grad_dec = dec_total.reshape(LATENTS, D)
    return (grad_enc, grad_dec, skip_total)
```

```python
import math

import jax
import jax.numpy as jnp
from jax import lax
from jax.sharding import PartitionSpec as P

BLK = 16


def gelu_pair(pre):
    factor = math.sqrt(2.0 / math.pi)
    inner = jnp.tanh(factor * (pre + 0.044715 * pre * pre * pre))
    value = 0.5 * pre * (1.0 + inner)
    slope = 0.5 * (1.0 + inner) + 0.5 * pre * (1.0 - inner * inner) * factor * (
        1.0 + 3.0 * 0.044715 * pre * pre
    )
    return (value, slope)


def local(
    inputs,
    target,
    enc_weight,
    enc_bias,
    dec_weight,
    dec_bias,
    skip_weight,
    block_ids,
    slot_lists,
    slot_counts,
):
    tok_rows, feat_dev = inputs.shape
    feat, lat_dev = enc_weight.shape
    owner = lax.axis_index("dict")
    n_dict = lax.axis_size("dict")
    n_tok = lax.axis_size("tok")
    scale = 1.0 / math.sqrt(tok_rows * n_tok)
    f32, bf16 = jnp.float32, jnp.bfloat16
    blocks = (owner * lat_dev + jnp.arange(lat_dev, dtype=jnp.int32)) // BLK
    active = jnp.any(block_ids[:, :, None] == blocks[None, None, :], axis=1)
    whole = lax.all_gather(inputs, "dict")
    dec_cols = lax.all_to_all(
        dec_weight.reshape(lat_dev, n_dict, feat_dev), "dict", split_axis=1, concat_axis=0, tiled=True
    ).reshape(n_dict * lat_dev, feat_dev)
    enc_blocks = enc_weight.reshape(n_dict, feat_dev, lat_dev)
    pre = jnp.einsum("btf,bfl->tl", whole, enc_blocks, preferred_element_type=f32) + enc_bias[None, :]
    value, slope = gelu_pair(pre)
    code = jnp.where(active, value, 0.0).astype(bf16)
    codes = lax.all_gather(code, "dict", axis=1, tiled=True)
    skip = jnp.einsum(
        "btf,bfm->tm", whole, skip_weight.reshape(n_dict, feat_dev, feat_dev), preferred_element_type=f32
    )
    recon = jnp.dot(codes, dec_cols, preferred_element_type=f32)
    err = recon + skip + dec_bias[None, :] - target.astype(f32)
    grad_out = (err * scale).astype(bf16)
    back = lax.dot_general(
        dec_cols, grad_out, (((1,), (1,)), ((), ())), preferred_element_type=f32
    ).astype(bf16)
    back = lax.all_to_all(
        back.reshape(n_dict, lat_dev, tok_rows), "dict", split_axis=0, concat_axis=0
    )
    skip_term = jnp.einsum("btf,tm->bfm", whole, grad_out, preferred_element_type=f32)
    skip_term = skip_term.reshape(feat, feat_dev).astype(bf16)
    grad_skip = lax.psum_scatter(skip_term, "tok", scatter_dimension=0, tiled=True).astype(f32)
    dec_term = lax.dot_general(
        codes, grad_out, (((0,), (0,)), ((), ())), preferred_element_type=f32
    ).astype(bf16)
    dec_term = lax.all_to_all(
        dec_term.reshape(n_dict, lat_dev, feat_dev), "dict", split_axis=0, concat_axis=0
    )
    dec_term = lax.psum_scatter(dec_term, "tok", scatter_dimension=0, tiled=True)
    grad_dec = dec_term.transpose(1, 0, 2).reshape(lat_dev, feat // n_tok).astype(f32)
    total = jnp.sum(back.astype(f32), axis=0).T
    dpre = jnp.where(active, total * slope, 0.0).astype(bf16)
    enc_term = jnp.einsum("btf,tl->bfl", whole, dpre, preferred_element_type=f32)
    enc_term = enc_term.reshape(feat, lat_dev).astype(bf16)
    grad_enc = lax.psum_scatter(enc_term, "tok", scatter_dimension=0, tiled=True).astype(f32)
    return (grad_enc, grad_dec, grad_skip)


def solution(mesh):
    in_specs = (
        P("tok", "dict"),
        P("tok", "dict"),
        P(None, "dict"),
        P("dict"),
        P("dict", None),
        P("dict"),
        P(None, "dict"),
        P("tok", None),
        P("tok", None, None),
        P("tok", None),
    )
    out_specs = (P("tok", "dict"), P("dict", "tok"), P("tok", "dict"))
    return jax.shard_map(local, mesh=mesh, in_specs=in_specs, out_specs=out_specs, check_vma=False)
```

```python
import functools
import math

import jax
import jax.numpy as jnp
from jax import lax
from jax.experimental import pallas as pl
from jax.experimental.pallas import tpu as pltpu
from jax.sharding import PartitionSpec as P

BLK = 16
MESH = pl.DeviceIdType.MESH


def gelu_pair(pre):
    factor = math.sqrt(2.0 / math.pi)
    inner = jnp.tanh(factor * (pre + 0.044715 * pre * pre * pre))
    value = 0.5 * pre * (1.0 + inner)
    slope = 0.5 * (1.0 + inner) + 0.5 * pre * (1.0 - inner * inner) * factor * (
        1.0 + 3.0 * 0.044715 * pre * pre
    )
    return (value, slope)


def dot(a, b, da, db):
    return lax.dot_general(a, b, (((da,), (db,)), ((), ())), preferred_element_type=jnp.float32)


def fused_kernel(
    nz, scale,
    xt, tt, enc, eb, dec, db, sw, ids,
    ge, gd, gs,
    encv, decv, swv, x_all, x_oth, dec_t, dec_cols, codes, go_all, go_oth, gd_part, gd_recv,
    dpre, dpre_oth, skip_acc, pre_acc, slope_s,
    load_sem, ag_send, ag_recv, xo_send, xo_fwd, xo_recv, dec_send, dec_recv, gd_send, gd_recv_sem,
    pair_send, pair_recv,
):
    f32, bf16 = jnp.float32, jnp.bfloat16
    n = 4 * nz
    nh = n // 2
    t, me = lax.axis_index("tok"), lax.axis_index("dict")
    z, y, c = me // 4, (me // 2) % 2, me % 2
    fd, lat = xt.shape[0], enc.shape[1]
    half = fd // 2

    def at(zz, yy, cc):
        return (zz * 2 + yy) * 2 + cc

    def rows(i, size):
        return pl.ds(pl.multiple_of(i * size, 16), size)

    sib, ypeer = (t, at(z, y, 1 - c)), (t, at(z, 1 - y, c))
    xpeer = (1 - t, me)
    zs = [(z + k) % nz for k in range(nz)]

    def copy(src, dst, s, r, dev):
        return pltpu.make_async_remote_copy(
            src_ref=src, dst_ref=dst, send_sem=s, recv_sem=r, device_id=dev, device_id_type=MESH
        )

    pending = []

    def send(src, dst, s, r, dev):
        cp = copy(src, dst, s, r, dev)
        cp.start()
        pending.append(cp)

    def arrived(ref, r):
        copy(ref, ref, pair_send.at[0], r, xpeer).wait_recv()

    def gather_own(p, buf, size):
        own = buf.at[rows(me, size)]
        for k in range(1, nz):
            send(own, own, ag_send.at[p, k - 1], ag_recv.at[p, me], (t, at(zs[k], y, c)))
        send(own, own, ag_send.at[p, nz - 1], ag_recv.at[p, me], ypeer)
        send(own, own, ag_send.at[p, nz], ag_recv.at[p, me], sib)

    def gather_z(p, buf, size, extra):
        extra(me, z)
        for k in range(1, nz):
            d = at(zs[nz - k], y, c)
            blk = buf.at[rows(d, size)]
            arrived(blk, ag_recv.at[p, d])
            send(blk, blk, ag_send.at[p, nz + 2 * k - 1], ag_recv.at[p, d], ypeer)
            send(blk, blk, ag_send.at[p, nz + 2 * k], ag_recv.at[p, d], sib)
            extra(d, zs[nz - k])

    def gather_y(p, buf, size, extra):
        for k in range(nz):
            d = at(zs[(nz - k) % nz], 1 - y, c)
            blk = buf.at[rows(d, size)]
            arrived(blk, ag_recv.at[p, d])
            send(blk, blk, ag_send.at[p, 3 * nz - 1 + k], ag_recv.at[p, d], sib)
            extra(d, zs[(nz - k) % nz])

    def nothing(d, zz):
        pass

    barrier = pltpu.get_barrier_semaphore()
    pl.semaphore_signal(barrier, inc=1, device_id=xpeer, device_id_type=MESH)
    for k in range(1, n):
        pl.semaphore_signal(barrier, inc=1, device_id=(t, (me + k) % n), device_id_type=MESH)
    loads = [
        pltpu.make_async_copy(s, d, load_sem.at[i])
        for i, (s, d) in enumerate(((dec, decv), (enc, encv), (sw, swv)))
    ]
    for cp in loads:
        cp.start()
    x_all[rows(me, fd), :] = xt[...]
    skip_acc[...] = jnp.zeros_like(skip_acc)
    pre_acc[...] = jnp.zeros_like(pre_acc)
    pl.semaphore_wait(barrier, n)

    gather_own(0, x_all, fd)
    loads[0].wait()
    width = dec_t.shape[1]
    for j in range(dec_t.shape[0] // width):
        dec_t[j * width : (j + 1) * width, :] = decv[:, j * width : (j + 1) * width].T

    def to_other(d, zz):
        @pl.when(zz // (nz // 2) == 1 - t)
        def _():
            j = d % nh
            copy(
                x_all.at[rows(d, fd)], x_oth.at[rows(j, fd)], xo_send.at[j], xo_recv.at[j], xpeer
            ).start()

    gather_z(0, x_all, fd, to_other)

    cols = pl.ds(pl.multiple_of(me * lat, 128), lat)
    part = pl.ds(pl.multiple_of(t * half, 16), half)
    for k in range(1, n):
        d = (me + k) % n
        send(
            dec_t.at[pl.ds(pl.multiple_of(d * fd + t * half, 16), half)],
            dec_cols.at[part, cols],
            dec_send.at[k - 1],
            dec_recv.at[me],
            (t, d),
        )
    dec_cols[part, cols] = dec_t[pl.ds(pl.multiple_of(me * fd + t * half, 16), half), :]
    loads[1].wait()
    loads[2].wait()

    def consume(d):
        r = rows(d, fd)
        blk = x_all[r, :]
        pre_acc[...] += dot(encv[r, :], blk, 0, 0)
        skip_acc[...] += dot(swv[r, :], blk, 0, 0)

    def line(yy, cc, use):
        def body(k, carry):
            use(at((z + nz - k) % nz, yy, cc))
            return carry

        lax.fori_loop(0, nz, body, 0)

    line(y, c, consume)
    gather_y(0, x_all, fd, to_other)
    line(1 - y, c, consume)

    def wait_consume(d):
        arrived(x_all.at[rows(d, fd)], ag_recv.at[0, d])
        consume(d)

    line(y, 1 - c, wait_consume)
    line(1 - y, 1 - c, wait_consume)

    pre = pre_acc[...] + eb[...]
    value, slope = gelu_pair(pre)
    blocks = lax.broadcasted_iota(jnp.int32, pre.shape, 0) // BLK + me * (lat // BLK)
    active = ids[0:1, :] == blocks
    for r in range(1, ids.shape[0]):
        active = active | (ids[r : r + 1, :] == blocks)
    slope_s[...] = jnp.where(active, slope, 0.0)
    code = jnp.where(active, value, 0.0).astype(bf16)
    codes[rows(me, lat), :] = code

    gather_own(1, codes, lat)
    gather_z(1, codes, lat, nothing)
    gather_y(1, codes, lat, nothing)
    for k in range(1, n):
        d = (me + k) % n
        arrived(dec_cols.at[part, pl.ds(pl.multiple_of(d * lat, 128), lat)], dec_recv.at[d])
    send(dec_cols.at[part], dec_cols.at[part], pair_send.at[1], pair_recv.at[1], xpeer)

    def wait_code(d):
        arrived(codes.at[rows(d, lat)], ag_recv.at[1, d])

    line(y, 1 - c, wait_code)
    line(1 - y, 1 - c, wait_code)
    arrived(dec_cols.at[pl.ds(pl.multiple_of((1 - t) * half, 16), half)], pair_recv.at[1])
    recon = dot(dec_cols[...], codes[...], 1, 0)
    err = recon + skip_acc[...] + db[...] - tt[...].astype(f32)
    go = (err * scale).astype(bf16)
    go_all[rows(me, fd), :] = go
    pre_acc[...] = jnp.zeros_like(pre_acc)

    own_go = go_all.at[rows(me, fd)]
    gather_own(2, go_all, fd)
    send(own_go, go_oth, pair_send.at[2], pair_recv.at[2], xpeer)
    gather_z(2, go_all, fd, nothing)

    def back(d):
        r = rows(d, fd)
        blk = go_all[r, :]
        pre_acc[...] += dot(dec_t[r, :], blk, 0, 0)
        gd_part[r, :] = dot(blk, codes[rows(me, lat), :], 1, 1).astype(bf16)

        @pl.when(d // nh == 1 - t)
        def _():
            j = d % nh
            copy(
                gd_part.at[r], gd_recv.at[rows(j, fd)], gd_send.at[j], gd_recv_sem.at[j], xpeer
            ).start()

    line(y, c, back)
    gather_y(2, go_all, fd, nothing)
    for zl in range(nz // 2):
        for yy in range(2):
            j = at(zl, yy, c)
            blk = x_oth.at[rows(j, fd)]
            arrived(blk, xo_recv.at[j])
            send(blk, blk, xo_fwd.at[zl * 2 + yy], xo_recv.at[j], sib)
    line(1 - y, c, back)

    def wait_back(d):
        arrived(go_all.at[rows(d, fd)], ag_recv.at[2, d])
        back(d)

    line(y, 1 - c, wait_back)
    line(1 - y, 1 - c, wait_back)
    dpre[...] = (pre_acc[...] * slope_s[...]).astype(bf16)
    send(dpre, dpre_oth, pair_send.at[3], pair_recv.at[3], xpeer)

    for zl in range(nz // 2):
        for yy in range(2):
            j = at(zl, yy, 1 - c)
            arrived(x_oth.at[rows(j, fd)], xo_recv.at[j])
    arrived(go_oth, pair_recv.at[2])

    def skip_rows(j, carry):
        r = rows(j, fd)
        mine = x_all[rows(t * nh + j, fd), :]
        gs[r, :] = dot(mine, go_all[rows(me, fd), :], 1, 1) + dot(x_oth[r, :], go_oth[...], 1, 1)
        return carry

    lax.fori_loop(0, nh, skip_rows, 0)
    arrived(dpre_oth, pair_recv.at[3])

    def enc_rows(j, carry):
        r = rows(j, fd)
        mine = x_all[rows(t * nh + j, fd), :]
        ge[r, :] = dot(mine, dpre[...], 1, 1) + dot(x_oth[r, :], dpre_oth[...], 1, 1)
        arrived(gd_recv.at[r], gd_recv_sem.at[j])
        gd[r, :] = gd_part[rows(t * nh + j, fd), :].astype(f32) + gd_recv[r, :].astype(f32)
        return carry

    lax.fori_loop(0, nh, enc_rows, 0)
    for cp in pending:
        cp.wait_send()
    for zl in range(nz // 2):
        for yy in range(2):
            j = at(zl, yy, c)
            blk = x_oth.at[rows(j, fd)]
            copy(blk, blk, xo_send.at[j], xo_recv.at[j], xpeer).wait_send()
    for j in range(nh):
        blk = gd_recv.at[rows(j, fd)]
        copy(blk, blk, gd_send.at[j], gd_recv_sem.at[j], xpeer).wait_send()


def fused(nz, inputs, target, enc_weight, enc_bias, dec_weight, dec_bias, skip_weight, block_ids):
    tok, fd = inputs.shape
    feat, lat = enc_weight.shape
    n = 4 * nz
    nh = n // 2
    f32, bf16 = jnp.float32, jnp.bfloat16
    vm, hbm = pl.BlockSpec(memory_space=pltpu.VMEM), pl.BlockSpec(memory_space=pl.ANY)
    sem = pltpu.SemaphoreType.DMA
    ge, gd, gs = pl.pallas_call(
        functools.partial(fused_kernel, nz, 1.0 / math.sqrt(2 * tok)),
        out_shape=(
            jax.ShapeDtypeStruct((feat // 2, lat), f32),
            jax.ShapeDtypeStruct((feat // 2, lat), f32),
            jax.ShapeDtypeStruct((feat // 2, fd), f32),
        ),
        in_specs=[vm, vm, hbm, vm, hbm, vm, hbm, vm],
        out_specs=(vm, vm, vm),
        scratch_shapes=[
            pltpu.VMEM((feat, lat), bf16),
            pltpu.VMEM((lat, feat), bf16),
            pltpu.VMEM((feat, fd), bf16),
            pltpu.VMEM((feat, tok), bf16),
            pltpu.VMEM((feat // 2, tok), bf16),
            pltpu.VMEM((feat, lat), bf16),
            pltpu.VMEM((fd, n * lat), bf16),
            pltpu.VMEM((n * lat, tok), bf16),
            pltpu.VMEM((feat, tok), bf16),
            pltpu.VMEM((fd, tok), bf16),
            pltpu.VMEM((feat, lat), bf16),
            pltpu.VMEM((feat // 2, lat), bf16),
            pltpu.VMEM((lat, tok), bf16),
            pltpu.VMEM((lat, tok), bf16),
            pltpu.VMEM((fd, tok), f32),
            pltpu.VMEM((lat, tok), f32),
            pltpu.VMEM((lat, tok), f32),
            sem((3,)),
            sem((3, 4 * nz)),
            sem((3, n)),
            sem((nh,)),
            sem((nz,)),
            sem((nh,)),
            sem((n - 1,)),
            sem((n,)),
            sem((nh,)),
            sem((nh,)),
            sem((4,)),
            sem((4,)),
        ],
        compiler_params=pltpu.CompilerParams(
            collective_id=0, has_side_effects=True, vmem_limit_bytes=58 * 1024 * 1024
        ),
    )(
        inputs.T, target.T, enc_weight, enc_bias[:, None], dec_weight, dec_bias[:, None],
        skip_weight, block_ids.T,
    )
    return (ge, gd.T, gs)


def local(
    inputs,
    target,
    enc_weight,
    enc_bias,
    dec_weight,
    dec_bias,
    skip_weight,
    block_ids,
    slot_lists,
    slot_counts,
):
    tok_rows, feat_dev = inputs.shape
    feat, lat_dev = enc_weight.shape
    owner = lax.axis_index("dict")
    n_dict = lax.axis_size("dict")
    n_tok = lax.axis_size("tok")
    nz = n_dict // 4
    aligned = tok_rows % 128 == 0 and feat_dev % 32 == 0 and lat_dev == 128
    if n_tok == 2 and nz % 2 == 0 and nz * 4 == n_dict and aligned:
        return fused(
            nz, inputs, target, enc_weight, enc_bias, dec_weight, dec_bias, skip_weight, block_ids
        )
    scale = 1.0 / math.sqrt(tok_rows * n_tok)
    f32, bf16 = jnp.float32, jnp.bfloat16
    blocks = (owner * lat_dev + jnp.arange(lat_dev, dtype=jnp.int32)) // BLK
    active = jnp.any(block_ids[:, :, None] == blocks[None, None, :], axis=1)
    whole = lax.all_gather(inputs, "dict")
    dec_cols = lax.all_to_all(
        dec_weight.reshape(lat_dev, n_dict, feat_dev), "dict", split_axis=1, concat_axis=0, tiled=True
    ).reshape(n_dict * lat_dev, feat_dev)
    enc_blocks = enc_weight.reshape(n_dict, feat_dev, lat_dev)
    pre = jnp.einsum("btf,bfl->tl", whole, enc_blocks, preferred_element_type=f32) + enc_bias[None, :]
    value, slope = gelu_pair(pre)
    code = jnp.where(active, value, 0.0).astype(bf16)
    codes = lax.all_gather(code, "dict", axis=1, tiled=True)
    skip = jnp.einsum(
        "btf,bfm->tm", whole, skip_weight.reshape(n_dict, feat_dev, feat_dev), preferred_element_type=f32
    )
    recon = jnp.dot(codes, dec_cols, preferred_element_type=f32)
    err = recon + skip + dec_bias[None, :] - target.astype(f32)
    grad_out = (err * scale).astype(bf16)
    back = lax.dot_general(
        dec_cols, grad_out, (((1,), (1,)), ((), ())), preferred_element_type=f32
    ).astype(bf16)
    back = lax.all_to_all(
        back.reshape(n_dict, lat_dev, tok_rows), "dict", split_axis=0, concat_axis=0
    )
    skip_term = jnp.einsum("btf,tm->bfm", whole, grad_out, preferred_element_type=f32)
    skip_term = skip_term.reshape(feat, feat_dev).astype(bf16)
    grad_skip = lax.psum_scatter(skip_term, "tok", scatter_dimension=0, tiled=True).astype(f32)
    dec_term = lax.dot_general(
        codes, grad_out, (((0,), (0,)), ((), ())), preferred_element_type=f32
    ).astype(bf16)
    dec_term = lax.all_to_all(
        dec_term.reshape(n_dict, lat_dev, feat_dev), "dict", split_axis=0, concat_axis=0
    )
    dec_term = lax.psum_scatter(dec_term, "tok", scatter_dimension=0, tiled=True)
    grad_dec = dec_term.transpose(1, 0, 2).reshape(lat_dev, feat // n_tok).astype(f32)
    total = jnp.sum(back.astype(f32), axis=0).T
    dpre = jnp.where(active, total * slope, 0.0).astype(bf16)
    enc_term = jnp.einsum("btf,tl->bfl", whole, dpre, preferred_element_type=f32)
    enc_term = enc_term.reshape(feat, lat_dev).astype(bf16)
    grad_enc = lax.psum_scatter(enc_term, "tok", scatter_dimension=0, tiled=True).astype(f32)
    return (grad_enc, grad_dec, grad_skip)


def solution(mesh):
    in_specs = (
        P("tok", "dict"),
        P("tok", "dict"),
        P(None, "dict"),
        P("dict"),
        P("dict", None),
        P("dict"),
        P(None, "dict"),
        P("tok", None),
        P("tok", None, None),
        P("tok", None),
    )
    out_specs = (P("tok", "dict"), P("dict", "tok"), P("tok", "dict"))
    return jax.shard_map(local, mesh=mesh, in_specs=in_specs, out_specs=out_specs, check_vma=False)
```

```python
import functools
import math

import jax
import jax.numpy as jnp
from jax import lax
from jax.experimental import pallas as pl
from jax.experimental.pallas import tpu as pltpu
from jax.sharding import PartitionSpec as P

BLK = 16
MESH = pl.DeviceIdType.MESH


def gelu_pair(pre):
    factor = math.sqrt(2.0 / math.pi)
    inner = jnp.tanh(factor * (pre + 0.044715 * pre * pre * pre))
    value = 0.5 * pre * (1.0 + inner)
    slope = 0.5 * (1.0 + inner) + 0.5 * pre * (1.0 - inner * inner) * factor * (
        1.0 + 3.0 * 0.044715 * pre * pre
    )
    return (value, slope)


def dot(a, b, da, db):
    return lax.dot_general(a, b, (((da,), (db,)), ((), ())), preferred_element_type=jnp.float32)


def fused_kernel(
    nz, scale,
    xt, tt, enc, eb, dec, db, sw, ids,
    ge, gd, gs,
    encv, decv, swv, x_all, x_oth, dec_t, dec_cols, codes, go_all, go_oth, gd_part, gd_recv,
    dpre, dpre_oth, skip_acc, pre_acc, slope_s,
    gs_v, load_sem, up_send, down_send, y_send, sib_send, ag_recv, dx_send, dx_recv, xo_send, xo_fwd, xo_recv, dec_send, dec_recv, gd_send, gd_recv_sem,
    pair_send, pair_recv,
):
    f32, bf16 = jnp.float32, jnp.bfloat16
    n = 4 * nz
    nh = n // 2
    t, me = lax.axis_index("tok"), lax.axis_index("dict")
    z, y, c = me // 4, (me // 2) % 2, me % 2
    fd, lat = xt.shape[0], enc.shape[1]
    half = fd // 2

    def at(zz, yy, cc):
        return (zz * 2 + yy) * 2 + cc

    def rows(i, size):
        return pl.ds(pl.multiple_of(i * size, 16), size)

    sib, ypeer = (t, at(z, y, 1 - c)), (t, at(z, 1 - y, c))
    xpeer = (1 - t, me)

    def copy(src, dst, s, r, dev):
        return pltpu.make_async_remote_copy(
            src_ref=src, dst_ref=dst, send_sem=s, recv_sem=r, device_id=dev, device_id_type=MESH
        )

    pending = []

    def send(src, dst, s, r, dev):
        cp = copy(src, dst, s, r, dev)
        cp.start()
        pending.append(cp)

    def arrived(ref, r):
        copy(ref, ref, pair_send.at[0], r, xpeer).wait_recv()

    def step(ref, s, r, dev):
        copy(ref, ref, s, r, dev).start()

    def pass_on(p, buf, size, zb):
        d = at(zb, y, c)
        blk = buf.at[rows(d, size)]
        step(blk, y_send.at[p, zb], ag_recv.at[p, d], ypeer)
        step(blk, sib_send.at[p, zb * 2 + y], ag_recv.at[p, d], sib)

    def chain(p, buf, size, zb, up):
        d = at(zb, y, c)
        blk = buf.at[rows(d, size)]

        @pl.when((z < nz - 1) if up else (z > 0))
        def _():
            to = (t, at(z + 1, y, c) if up else at(z - 1, y, c))
            step(blk, (up_send if up else down_send).at[p, zb], ag_recv.at[p, d], to)

    def gather_own(p, buf, size):
        chain(p, buf, size, z, True)
        chain(p, buf, size, z, False)
        pass_on(p, buf, size, z)

    def gather_z(p, buf, size, extra, between=lambda k: None):
        extra(me, z)
        for k in range(1, nz):
            for up in (True, False):
                zb = z - k if up else z + k

                @pl.when((zb >= 0) if up else (zb < nz))
                def _():
                    d = at(zb, y, c)
                    arrived(buf.at[rows(d, size)], ag_recv.at[p, d])
                    chain(p, buf, size, zb, up)
                    pass_on(p, buf, size, zb)
                    extra(d, zb)

            between(k)

    def gather_y(p, buf, size, extra):
        def forward(zb):
            d = at(zb, 1 - y, c)
            blk = buf.at[rows(d, size)]
            arrived(blk, ag_recv.at[p, d])
            step(blk, sib_send.at[p, zb * 2 + 1 - y], ag_recv.at[p, d], sib)
            extra(d, zb)

        forward(z)
        for k in range(1, nz):
            for up in (True, False):
                zb = z - k if up else z + k

                @pl.when((zb >= 0) if up else (zb < nz))
                def _():
                    forward(zb)

    def drain(p, buf, size):
        blk = buf.at[rows(me, size)]

        def sent(s):
            copy(blk, blk, s, ag_recv.at[p, me], sib).wait_send()

        for zb in range(nz):
            sent(y_send.at[p, zb])
            sent(sib_send.at[p, zb * 2])
            sent(sib_send.at[p, zb * 2 + 1])
            if zb < nz - 1:
                @pl.when((zb <= z) & (z < nz - 1))
                def _():
                    sent(up_send.at[p, zb])
            if zb > 0:
                @pl.when((zb >= z) & (z > 0))
                def _():
                    sent(down_send.at[p, zb])

    def nothing(d, zz):
        pass

    barrier = pltpu.get_barrier_semaphore()
    pl.semaphore_signal(barrier, inc=1, device_id=xpeer, device_id_type=MESH)
    for k in range(1, n):
        pl.semaphore_signal(barrier, inc=1, device_id=(t, (me + k) % n), device_id_type=MESH)
    loads = [
        pltpu.make_async_copy(s, d, load_sem.at[i])
        for i, (s, d) in enumerate(((dec, decv), (enc, encv), (sw, swv)))
    ]
    for cp in loads:
        cp.start()
    x_all[rows(me, fd), :] = xt[...]
    pre_acc[...] = jnp.zeros_like(pre_acc)
    pl.semaphore_wait(barrier, n)

    gather_own(0, x_all, fd)
    loads[0].wait()
    width = dec_t.shape[1]
    for j in range(dec_t.shape[0] // width):
        dec_t[j * width : (j + 1) * width, :] = decv[:, j * width : (j + 1) * width].T

    def to_other(d, zz):
        @pl.when(zz // (nz // 2) == 1 - t)
        def _():
            j = d % nh
            copy(
                x_all.at[rows(d, fd)], x_oth.at[rows(j, fd)], xo_send.at[j], xo_recv.at[j], xpeer
            ).start()

    gather_z(0, x_all, fd, to_other)

    cols = pl.ds(pl.multiple_of(me * lat, 128), lat)
    part = pl.ds(pl.multiple_of(t * half, 16), half)
    for k in range(1, n):
        d = (me + k) % n
        send(
            dec_t.at[pl.ds(pl.multiple_of(d * fd + t * half, 16), half)],
            dec_cols.at[part, cols],
            dec_send.at[k - 1],
            dec_recv.at[me],
            (t, d),
        )
    dec_cols[part, cols] = dec_t[pl.ds(pl.multiple_of(me * fd + t * half, 16), half), :]
    loads[1].wait()

    def consume(d):
        r = rows(d, fd)
        blk = x_all[r, :]
        pre_acc[...] += dot(encv[r, :], blk, 0, 0)

    def line(yy, cc, use):
        def body(k, carry):
            use(at((z + nz - k) % nz, yy, cc))
            return carry

        lax.fori_loop(0, nz, body, 0)

    line(y, c, consume)
    gather_y(0, x_all, fd, to_other)
    line(1 - y, c, consume)

    def wait_consume(d):
        arrived(x_all.at[rows(d, fd)], ag_recv.at[0, d])
        consume(d)

    line(y, 1 - c, wait_consume)
    line(1 - y, 1 - c, wait_consume)

    def column(row):
        size = row.shape[1]
        eye = lax.broadcasted_iota(jnp.int32, (size, size), 0) == lax.broadcasted_iota(
            jnp.int32, (size, size), 1
        )
        return jnp.sum(jnp.where(eye, row, 0.0), axis=1, keepdims=True)

    pre = pre_acc[...] + column(eb[...])
    value, slope = gelu_pair(pre)
    blocks = lax.broadcasted_iota(jnp.int32, pre.shape, 0) // BLK + me * (lat // BLK)
    active = ids[0:1, :] == blocks
    for r in range(1, ids.shape[0]):
        active = active | (ids[r : r + 1, :] == blocks)
    slope_s[...] = jnp.where(active, slope, 0.0)
    code = jnp.where(active, value, 0.0).astype(bf16)
    codes[rows(me, lat), :] = code

    gather_own(1, codes, lat)
    loads[2].wait()
    wide = 512 if swv.shape[1] % 512 == 0 else 128
    skip_acc[...] = column(db[...]) - tt[...].astype(f32)

    def skip_cols(j, carry):
        r = pl.ds(pl.multiple_of(j * wide, 128), wide)
        skip_acc[...] += dot(swv[:, r], x_all[r, :], 1, 0)
        return carry

    lax.fori_loop(0, swv.shape[1] // wide, skip_cols, 0)

    def dec_to_other(k):
        if k == 1:
            for i in range(n):
                d = (me + i) % n
                blk = dec_cols.at[part, pl.ds(pl.multiple_of(d * lat, 128), lat)]
                if i:
                    arrived(blk, dec_recv.at[d])
                send(blk, blk, dx_send.at[i], dx_recv.at[d], xpeer)

    gather_z(1, codes, lat, nothing, dec_to_other)
    gather_y(1, codes, lat, nothing)

    def wait_code(d):
        arrived(codes.at[rows(d, lat)], ag_recv.at[1, d])

    line(y, 1 - c, wait_code)
    line(1 - y, 1 - c, wait_code)
    other = pl.ds(pl.multiple_of((1 - t) * half, 16), half)
    for d in range(n):
        arrived(dec_cols.at[other, d * lat : (d + 1) * lat], dx_recv.at[d])
    err = dot(dec_cols[...], codes[...], 1, 0) + skip_acc[...]
    go = (err * scale).astype(bf16)
    go_all[rows(me, fd), :] = go
    pre_acc[...] = jnp.zeros_like(pre_acc)

    own_go = go_all.at[rows(me, fd)]
    gather_own(2, go_all, fd)
    send(own_go, go_oth, pair_send.at[2], pair_recv.at[2], xpeer)
    for zl in range(nz // 2):
        for yy in range(2):
            j = at(zl, yy, c)
            blk = x_oth.at[rows(j, fd)]
            arrived(blk, xo_recv.at[j])
            send(blk, blk, xo_fwd.at[zl * 2 + yy], xo_recv.at[j], sib)
    tall = 256 if gs_v.shape[1] % 256 == 0 else 128
    gs_copy = pltpu.make_async_copy(gs_v, gs, load_sem.at[3])

    def grad_skip(k):
        if k == max(1, nz - 2):
            for zl in range(nz // 2):
                for yy in range(2):
                    j = at(zl, yy, 1 - c)
                    arrived(x_oth.at[rows(j, fd)], xo_recv.at[j])
            arrived(go_oth, pair_recv.at[2])

            def body(j, carry):
                r = pl.ds(pl.multiple_of(j * tall, 128), tall)
                mine = x_all[pl.ds(pl.multiple_of(t * nh * fd + j * tall, 16), tall), :]
                gs_v[:, r] = dot(go_all[rows(me, fd), :], mine, 1, 1) + dot(
                    go_oth[...], x_oth[r, :], 1, 1
                )
                return carry

            lax.fori_loop(0, gs_v.shape[1] // tall, body, 0)
            gs_copy.start()

    gather_z(2, go_all, fd, nothing, grad_skip)

    def back(d):
        r = rows(d, fd)
        blk = go_all[r, :]
        pre_acc[...] += dot(dec_t[r, :], blk, 0, 0)
        gd_part[r, :] = dot(blk, codes[rows(me, lat), :], 1, 1).astype(bf16)

        @pl.when(d // nh == 1 - t)
        def _():
            j = d % nh
            copy(
                gd_part.at[r], gd_recv.at[rows(j, fd)], gd_send.at[j], gd_recv_sem.at[j], xpeer
            ).start()

    line(y, c, back)
    gather_y(2, go_all, fd, nothing)
    line(1 - y, c, back)

    def wait_back(d):
        arrived(go_all.at[rows(d, fd)], ag_recv.at[2, d])
        back(d)

    line(y, 1 - c, wait_back)
    line(1 - y, 1 - c, wait_back)
    dpre[...] = (pre_acc[...] * slope_s[...]).astype(bf16)
    send(dpre, dpre_oth, pair_send.at[3], pair_recv.at[3], xpeer)


    def dec_rows(j, carry):
        r = rows(j, fd)
        arrived(gd_recv.at[r], gd_recv_sem.at[j])
        gd[r, :] = gd_part[rows(t * nh + j, fd), :].astype(f32) + gd_recv[r, :].astype(f32)
        return carry

    lax.fori_loop(0, nh, dec_rows, 0)
    arrived(dpre_oth, pair_recv.at[3])

    def enc_rows(j, carry):
        r = rows(j, fd)
        mine = x_all[rows(t * nh + j, fd), :]
        ge[r, :] = dot(mine, dpre[...], 1, 1) + dot(x_oth[r, :], dpre_oth[...], 1, 1)
        return carry

    lax.fori_loop(0, nh, enc_rows, 0)
    gs_copy.wait()
    drain(0, x_all, fd)
    drain(1, codes, lat)
    drain(2, go_all, fd)
    for cp in pending:
        cp.wait_send()
    for zl in range(nz // 2):
        for yy in range(2):
            j = at(zl, yy, c)
            blk = x_oth.at[rows(j, fd)]
            copy(blk, blk, xo_send.at[j], xo_recv.at[j], xpeer).wait_send()
    for j in range(nh):
        blk = gd_recv.at[rows(j, fd)]
        copy(blk, blk, gd_send.at[j], gd_recv_sem.at[j], xpeer).wait_send()


def fused(nz, inputs, target, enc_weight, enc_bias, dec_weight, dec_bias, skip_weight, block_ids):
    tok, fd = inputs.shape
    feat, lat = enc_weight.shape
    n = 4 * nz
    nh = n // 2
    f32, bf16 = jnp.float32, jnp.bfloat16
    vm, hbm = pl.BlockSpec(memory_space=pltpu.VMEM), pl.BlockSpec(memory_space=pl.ANY)
    sem = pltpu.SemaphoreType.DMA
    ge, gd, gs = pl.pallas_call(
        functools.partial(fused_kernel, nz, 1.0 / math.sqrt(2 * tok)),
        out_shape=(
            jax.ShapeDtypeStruct((feat // 2, lat), f32),
            jax.ShapeDtypeStruct((feat // 2, lat), f32),
            jax.ShapeDtypeStruct((fd, feat // 2), f32),
        ),
        in_specs=[vm, vm, hbm, vm, hbm, vm, hbm, vm],
        out_specs=(vm, vm, hbm),
        scratch_shapes=[
            pltpu.VMEM((feat, lat), bf16),
            pltpu.VMEM((lat, feat), bf16),
            pltpu.VMEM((fd, feat), bf16),
            pltpu.VMEM((feat, tok), bf16),
            pltpu.VMEM((feat // 2, tok), bf16),
            pltpu.VMEM((feat, lat), bf16),
            pltpu.VMEM((fd, n * lat), bf16),
            pltpu.VMEM((n * lat, tok), bf16),
            pltpu.VMEM((feat, tok), bf16),
            pltpu.VMEM((fd, tok), bf16),
            pltpu.VMEM((feat, lat), bf16),
            pltpu.VMEM((feat // 2, lat), bf16),
            pltpu.VMEM((lat, tok), bf16),
            pltpu.VMEM((lat, tok), bf16),
            pltpu.VMEM((fd, tok), f32),
            pltpu.VMEM((lat, tok), f32),
            pltpu.VMEM((lat, tok), f32),
            pltpu.VMEM((fd, feat // 2), f32),
            sem((4,)),
            sem((3, nz)),
            sem((3, nz)),
            sem((3, nz)),
            sem((3, 2 * nz)),
            sem((3, n)),
            sem((n,)),
            sem((n,)),
            sem((nh,)),
            sem((nz,)),
            sem((nh,)),
            sem((n - 1,)),
            sem((n,)),
            sem((nh,)),
            sem((nh,)),
            sem((4,)),
            sem((4,)),
        ],
        compiler_params=pltpu.CompilerParams(
            collective_id=0, has_side_effects=True, vmem_limit_bytes=58 * 1024 * 1024
        ),
    )(
        inputs.T, target.T, enc_weight, enc_bias[None, :], dec_weight, dec_bias[None, :],
        skip_weight.T, block_ids.T,
    )
    return (ge, gd.T, gs.T)


def local(
    inputs,
    target,
    enc_weight,
    enc_bias,
    dec_weight,
    dec_bias,
    skip_weight,
    block_ids,
    slot_lists,
    slot_counts,
):
    tok_rows, feat_dev = inputs.shape
    feat, lat_dev = enc_weight.shape
    owner = lax.axis_index("dict")
    n_dict = lax.axis_size("dict")
    n_tok = lax.axis_size("tok")
    nz = n_dict // 4
    aligned = tok_rows % 128 == 0 and enc_weight.shape[0] % 256 == 0 and feat_dev % 32 == 0 and lat_dev == 128
    if n_tok == 2 and nz % 2 == 0 and nz * 4 == n_dict and aligned:
        return fused(
            nz, inputs, target, enc_weight, enc_bias, dec_weight, dec_bias, skip_weight, block_ids
        )
    scale = 1.0 / math.sqrt(tok_rows * n_tok)
    f32, bf16 = jnp.float32, jnp.bfloat16
    blocks = (owner * lat_dev + jnp.arange(lat_dev, dtype=jnp.int32)) // BLK
    active = jnp.any(block_ids[:, :, None] == blocks[None, None, :], axis=1)
    whole = lax.all_gather(inputs, "dict")
    dec_cols = lax.all_to_all(
        dec_weight.reshape(lat_dev, n_dict, feat_dev), "dict", split_axis=1, concat_axis=0, tiled=True
    ).reshape(n_dict * lat_dev, feat_dev)
    enc_blocks = enc_weight.reshape(n_dict, feat_dev, lat_dev)
    pre = jnp.einsum("btf,bfl->tl", whole, enc_blocks, preferred_element_type=f32) + enc_bias[None, :]
    value, slope = gelu_pair(pre)
    code = jnp.where(active, value, 0.0).astype(bf16)
    codes = lax.all_gather(code, "dict", axis=1, tiled=True)
    skip = jnp.einsum(
        "btf,bfm->tm", whole, skip_weight.reshape(n_dict, feat_dev, feat_dev), preferred_element_type=f32
    )
    recon = jnp.dot(codes, dec_cols, preferred_element_type=f32)
    err = recon + skip + dec_bias[None, :] - target.astype(f32)
    grad_out = (err * scale).astype(bf16)
    back = lax.dot_general(
        dec_cols, grad_out, (((1,), (1,)), ((), ())), preferred_element_type=f32
    ).astype(bf16)
    back = lax.all_to_all(
        back.reshape(n_dict, lat_dev, tok_rows), "dict", split_axis=0, concat_axis=0
    )
    skip_term = jnp.einsum("btf,tm->bfm", whole, grad_out, preferred_element_type=f32)
    skip_term = skip_term.reshape(feat, feat_dev).astype(bf16)
    grad_skip = lax.psum_scatter(skip_term, "tok", scatter_dimension=0, tiled=True).astype(f32)
    dec_term = lax.dot_general(
        codes, grad_out, (((0,), (0,)), ((), ())), preferred_element_type=f32
    ).astype(bf16)
    dec_term = lax.all_to_all(
        dec_term.reshape(n_dict, lat_dev, feat_dev), "dict", split_axis=0, concat_axis=0
    )
    dec_term = lax.psum_scatter(dec_term, "tok", scatter_dimension=0, tiled=True)
    grad_dec = dec_term.transpose(1, 0, 2).reshape(lat_dev, feat // n_tok).astype(f32)
    total = jnp.sum(back.astype(f32), axis=0).T
    dpre = jnp.where(active, total * slope, 0.0).astype(bf16)
    enc_term = jnp.einsum("btf,tl->bfl", whole, dpre, preferred_element_type=f32)
    enc_term = enc_term.reshape(feat, lat_dev).astype(bf16)
    grad_enc = lax.psum_scatter(enc_term, "tok", scatter_dimension=0, tiled=True).astype(f32)
    return (grad_enc, grad_dec, grad_skip)


def solution(mesh):
    in_specs = (
        P("tok", "dict"),
        P("tok", "dict"),
        P(None, "dict"),
        P("dict"),
        P("dict", None),
        P("dict"),
        P(None, "dict"),
        P("tok", None),
        P("tok", None, None),
        P("tok", None),
    )
    out_specs = (P("tok", "dict"), P("dict", "tok"), P("tok", "dict"))
    return jax.shard_map(local, mesh=mesh, in_specs=in_specs, out_specs=out_specs, check_vma=False)
```

```python
import functools
import math

import jax
import jax.numpy as jnp
from jax import lax
from jax.experimental import pallas as pl
from jax.experimental.pallas import tpu as pltpu
from jax.sharding import PartitionSpec as P

BLK = 16
MESH = pl.DeviceIdType.MESH


def gelu_pair(pre):
    factor = math.sqrt(2.0 / math.pi)
    inner = jnp.tanh(factor * (pre + 0.044715 * pre * pre * pre))
    value = 0.5 * pre * (1.0 + inner)
    slope = 0.5 * (1.0 + inner) + 0.5 * pre * (1.0 - inner * inner) * factor * (
        1.0 + 3.0 * 0.044715 * pre * pre
    )
    return (value, slope)


def dot(a, b, da, db):
    return lax.dot_general(a, b, (((da,), (db,)), ((), ())), preferred_element_type=jnp.float32)


def fused_kernel(
    nz, scale,
    xt, tt, enc, eb, dec, db, sw, ids,
    ge, gd, gs,
    encv, decv, swv, x_all, x_oth, dec_t, dec_cols, codes, go_all, go_oth, gd_part, gd_recv,
    dpre, dpre_oth, skip_acc, pre_acc, slope_s,
    gs_v, load_sem, up_send, down_send, y_send, sib_send, ag_recv, dx_send, dx_recv, xo_send, xo_fwd, xo_recv, dec_send, dec_recv, gd_send, gd_recv_sem,
    pair_send, pair_recv,
):
    f32, bf16 = jnp.float32, jnp.bfloat16
    n = 4 * nz
    nh = n // 2
    t, me = lax.axis_index("tok"), lax.axis_index("dict")
    z, y, c = me // 4, (me // 2) % 2, me % 2
    fd, lat = xt.shape[0], enc.shape[1]
    half = fd // 2

    def at(zz, yy, cc):
        return (zz * 2 + yy) * 2 + cc

    def rows(i, size):
        return pl.ds(pl.multiple_of(i * size, 16), size)

    sib, ypeer = (t, at(z, y, 1 - c)), (t, at(z, 1 - y, c))
    xpeer = (1 - t, me)

    def copy(src, dst, s, r, dev):
        return pltpu.make_async_remote_copy(
            src_ref=src, dst_ref=dst, send_sem=s, recv_sem=r, device_id=dev, device_id_type=MESH
        )

    pending = []

    def send(src, dst, s, r, dev):
        cp = copy(src, dst, s, r, dev)
        cp.start()
        pending.append(cp)

    def arrived(ref, r):
        copy(ref, ref, pair_send.at[0], r, xpeer).wait_recv()

    def step(ref, s, r, dev):
        copy(ref, ref, s, r, dev).start()

    def pass_on(p, buf, size, zb):
        d = at(zb, y, c)
        blk = buf.at[rows(d, size)]
        step(blk, y_send.at[p, zb], ag_recv.at[p, d], ypeer)
        step(blk, sib_send.at[p, zb * 2 + y], ag_recv.at[p, d], sib)

    def chain(p, buf, size, zb, up):
        d = at(zb, y, c)
        blk = buf.at[rows(d, size)]

        @pl.when((z < nz - 1) if up else (z > 0))
        def _():
            to = (t, at(z + 1, y, c) if up else at(z - 1, y, c))
            step(blk, (up_send if up else down_send).at[p, zb], ag_recv.at[p, d], to)

    def gather_own(p, buf, size):
        chain(p, buf, size, z, True)
        chain(p, buf, size, z, False)
        pass_on(p, buf, size, z)

    def at_step(k, use):
        if k == 0:
            use(z, True)
            return
        for up in (True, False):
            zb = z - k if up else z + k

            @pl.when((zb >= 0) if up else (zb < nz))
            def _():
                use(zb, up)

    def gather(p, buf, size, extra, consume, between=lambda k: None):
        def from_z(zb, up):
            d = at(zb, y, c)
            arrived(buf.at[rows(d, size)], ag_recv.at[p, d])
            chain(p, buf, size, zb, up)
            pass_on(p, buf, size, zb)
            extra(d, zb)

        def from_y(zb, up):
            d = at(zb, 1 - y, c)
            blk = buf.at[rows(d, size)]
            arrived(blk, ag_recv.at[p, d])
            step(blk, sib_send.at[p, zb * 2 + 1 - y], ag_recv.at[p, d], sib)
            extra(d, zb)

        def near(zb, up):
            consume(at(zb, y, c))
            other = at(zb, y, 1 - c)
            arrived(buf.at[rows(other, size)], ag_recv.at[p, other])
            consume(other)

        def far(zb, up):
            consume(at(zb, 1 - y, c))
            other = at(zb, 1 - y, 1 - c)
            arrived(buf.at[rows(other, size)], ag_recv.at[p, other])
            consume(other)

        extra(me, z)
        for k in range(1, nz + 2):
            if k < nz:
                at_step(k, from_z)
            if k <= nz:
                at_step(k - 1, from_y)
            between(k)
            if k <= nz:
                at_step(k - 1, near)
            if k > 1:
                at_step(k - 2, far)

    def drain(p, buf, size):
        blk = buf.at[rows(me, size)]

        def sent(s):
            copy(blk, blk, s, ag_recv.at[p, me], sib).wait_send()

        for zb in range(nz):
            sent(y_send.at[p, zb])
            sent(sib_send.at[p, zb * 2])
            sent(sib_send.at[p, zb * 2 + 1])
            if zb < nz - 1:
                @pl.when((zb <= z) & (z < nz - 1))
                def _():
                    sent(up_send.at[p, zb])
            if zb > 0:
                @pl.when((zb >= z) & (z > 0))
                def _():
                    sent(down_send.at[p, zb])

    def nothing(d, zz):
        pass

    barrier = pltpu.get_barrier_semaphore()
    pl.semaphore_signal(barrier, inc=1, device_id=xpeer, device_id_type=MESH)
    for k in range(1, n):
        pl.semaphore_signal(barrier, inc=1, device_id=(t, (me + k) % n), device_id_type=MESH)
    loads = [
        pltpu.make_async_copy(s, d, load_sem.at[i])
        for i, (s, d) in enumerate(((dec, decv), (enc, encv), (sw, swv)))
    ]
    for cp in loads:
        cp.start()
    x_all[rows(me, fd), :] = xt[...]
    pre_acc[...] = jnp.zeros_like(pre_acc)
    pl.semaphore_wait(barrier, n)

    gather_own(0, x_all, fd)
    loads[0].wait()
    width = dec_t.shape[1]
    for j in range(dec_t.shape[0] // width):
        dec_t[j * width : (j + 1) * width, :] = decv[:, j * width : (j + 1) * width].T

    def to_other(d, zz):
        @pl.when(zz // (nz // 2) == 1 - t)
        def _():
            j = d % nh
            copy(
                x_all.at[rows(d, fd)], x_oth.at[rows(j, fd)], xo_send.at[j], xo_recv.at[j], xpeer
            ).start()

    cols = pl.ds(pl.multiple_of(me * lat, 128), lat)
    part = pl.ds(pl.multiple_of(t * half, 16), half)

    def dec_columns(k):
        if k != max(1, nz - 2):
            return
        for i in range(1, n):
            d = (me + i) % n
            send(
                dec_t.at[pl.ds(pl.multiple_of(d * fd + t * half, 16), half)],
                dec_cols.at[part, cols],
                dec_send.at[i - 1],
                dec_recv.at[me],
                (t, d),
            )
        dec_cols[part, cols] = dec_t[pl.ds(pl.multiple_of(me * fd + t * half, 16), half), :]

    loads[1].wait()

    def consume(d):
        r = rows(d, fd)
        blk = x_all[r, :]
        pre_acc[...] += dot(encv[r, :], blk, 0, 0)

    gather(0, x_all, fd, to_other, consume, dec_columns)

    def column(row):
        size = row.shape[1]
        eye = lax.broadcasted_iota(jnp.int32, (size, size), 0) == lax.broadcasted_iota(
            jnp.int32, (size, size), 1
        )
        return jnp.sum(jnp.where(eye, row, 0.0), axis=1, keepdims=True)

    pre = pre_acc[...] + column(eb[...])
    value, slope = gelu_pair(pre)
    blocks = lax.broadcasted_iota(jnp.int32, pre.shape, 0) // BLK + me * (lat // BLK)
    active = ids[0:1, :] == blocks
    for r in range(1, ids.shape[0]):
        active = active | (ids[r : r + 1, :] == blocks)
    slope_s[...] = jnp.where(active, slope, 0.0)
    code = jnp.where(active, value, 0.0).astype(bf16)
    codes[rows(me, lat), :] = code

    gather_own(1, codes, lat)
    loads[2].wait()
    wide = 512 if swv.shape[1] % 512 == 0 else 128
    skip_acc[...] = column(db[...]) - tt[...].astype(f32)

    def skip_cols(j, carry):
        r = pl.ds(pl.multiple_of(j * wide, 128), wide)
        skip_acc[...] += dot(swv[:, r], x_all[r, :], 1, 0)
        return carry

    lax.fori_loop(0, swv.shape[1] // wide, skip_cols, 0)

    def dec_to_other(k):
        if k == 1:
            for i in range(n):
                d = (me + i) % n
                blk = dec_cols.at[part, pl.ds(pl.multiple_of(d * lat, 128), lat)]
                if i:
                    arrived(blk, dec_recv.at[d])
                send(blk, blk, dx_send.at[i], dx_recv.at[d], xpeer)

    gather(1, codes, lat, nothing, lambda d: None, dec_to_other)
    other = pl.ds(pl.multiple_of((1 - t) * half, 16), half)
    for d in range(n):
        arrived(dec_cols.at[other, d * lat : (d + 1) * lat], dx_recv.at[d])
    err = dot(dec_cols[...], codes[...], 1, 0) + skip_acc[...]
    go = (err * scale).astype(bf16)
    go_all[rows(me, fd), :] = go
    pre_acc[...] = jnp.zeros_like(pre_acc)

    own_go = go_all.at[rows(me, fd)]
    gather_own(2, go_all, fd)
    send(own_go, go_oth, pair_send.at[2], pair_recv.at[2], xpeer)
    for zl in range(nz // 2):
        for yy in range(2):
            j = at(zl, yy, c)
            blk = x_oth.at[rows(j, fd)]
            arrived(blk, xo_recv.at[j])
            send(blk, blk, xo_fwd.at[zl * 2 + yy], xo_recv.at[j], sib)
    tall = 256 if gs_v.shape[1] % 256 == 0 else 128
    gs_copy = pltpu.make_async_copy(gs_v, gs, load_sem.at[3])

    def grad_skip(k):
        if k == max(1, nz - 2):
            for zl in range(nz // 2):
                for yy in range(2):
                    j = at(zl, yy, 1 - c)
                    arrived(x_oth.at[rows(j, fd)], xo_recv.at[j])
            arrived(go_oth, pair_recv.at[2])

            def body(j, carry):
                r = pl.ds(pl.multiple_of(j * tall, 128), tall)
                mine = x_all[pl.ds(pl.multiple_of(t * nh * fd + j * tall, 16), tall), :]
                gs_v[:, r] = dot(go_all[rows(me, fd), :], mine, 1, 1) + dot(
                    go_oth[...], x_oth[r, :], 1, 1
                )
                return carry

            lax.fori_loop(0, gs_v.shape[1] // tall, body, 0)
            gs_copy.start()

    def back(d):
        r = rows(d, fd)
        blk = go_all[r, :]
        pre_acc[...] += dot(dec_t[r, :], blk, 0, 0)
        gd_part[r, :] = dot(blk, codes[rows(me, lat), :], 1, 1).astype(bf16)

        @pl.when(d // nh == 1 - t)
        def _():
            j = d % nh
            copy(
                gd_part.at[r], gd_recv.at[rows(j, fd)], gd_send.at[j], gd_recv_sem.at[j], xpeer
            ).start()

    gather(2, go_all, fd, nothing, back, grad_skip)
    dpre[...] = (pre_acc[...] * slope_s[...]).astype(bf16)
    send(dpre, dpre_oth, pair_send.at[3], pair_recv.at[3], xpeer)


    for j in range(nh):
        arrived(gd_recv.at[rows(j, fd)], gd_recv_sem.at[j])

    def dec_rows(j, carry):
        r = rows(j, lat)
        mine = gd_part[pl.ds(pl.multiple_of(t * nh * fd + j * lat, 16), lat), :]
        total = mine.astype(f32) + gd_recv[r, :].astype(f32)
        gd[:, pl.ds(pl.multiple_of(j * lat, 128), lat)] = total.T
        return carry

    lax.fori_loop(0, nh * fd // lat, dec_rows, 0)
    arrived(dpre_oth, pair_recv.at[3])

    def enc_rows(j, carry):
        r = rows(j, fd)
        mine = x_all[rows(t * nh + j, fd), :]
        ge[r, :] = dot(mine, dpre[...], 1, 1) + dot(x_oth[r, :], dpre_oth[...], 1, 1)
        return carry

    lax.fori_loop(0, nh, enc_rows, 0)
    gs_copy.wait()
    drain(0, x_all, fd)
    drain(1, codes, lat)
    drain(2, go_all, fd)
    for cp in pending:
        cp.wait_send()
    for zl in range(nz // 2):
        for yy in range(2):
            j = at(zl, yy, c)
            blk = x_oth.at[rows(j, fd)]
            copy(blk, blk, xo_send.at[j], xo_recv.at[j], xpeer).wait_send()
    for j in range(nh):
        blk = gd_recv.at[rows(j, fd)]
        copy(blk, blk, gd_send.at[j], gd_recv_sem.at[j], xpeer).wait_send()


def fused(nz, inputs, target, enc_weight, enc_bias, dec_weight, dec_bias, skip_weight, block_ids):
    tok, fd = inputs.shape
    feat, lat = enc_weight.shape
    n = 4 * nz
    nh = n // 2
    f32, bf16 = jnp.float32, jnp.bfloat16
    vm, hbm = pl.BlockSpec(memory_space=pltpu.VMEM), pl.BlockSpec(memory_space=pl.ANY)
    sem = pltpu.SemaphoreType.DMA
    ge, gd, gs = pl.pallas_call(
        functools.partial(fused_kernel, nz, 1.0 / math.sqrt(2 * tok)),
        out_shape=(
            jax.ShapeDtypeStruct((feat // 2, lat), f32),
            jax.ShapeDtypeStruct((lat, feat // 2), f32),
            jax.ShapeDtypeStruct((fd, feat // 2), f32),
        ),
        in_specs=[vm, vm, hbm, vm, hbm, vm, hbm, vm],
        out_specs=(vm, vm, hbm),
        scratch_shapes=[
            pltpu.VMEM((feat, lat), bf16),
            pltpu.VMEM((lat, feat), bf16),
            pltpu.VMEM((fd, feat), bf16),
            pltpu.VMEM((feat, tok), bf16),
            pltpu.VMEM((feat // 2, tok), bf16),
            pltpu.VMEM((feat, lat), bf16),
            pltpu.VMEM((fd, n * lat), bf16),
            pltpu.VMEM((n * lat, tok), bf16),
            pltpu.VMEM((feat, tok), bf16),
            pltpu.VMEM((fd, tok), bf16),
            pltpu.VMEM((feat, lat), bf16),
            pltpu.VMEM((feat // 2, lat), bf16),
            pltpu.VMEM((lat, tok), bf16),
            pltpu.VMEM((lat, tok), bf16),
            pltpu.VMEM((fd, tok), f32),
            pltpu.VMEM((lat, tok), f32),
            pltpu.VMEM((lat, tok), f32),
            pltpu.VMEM((fd, feat // 2), f32),
            sem((4,)),
            sem((3, nz)),
            sem((3, nz)),
            sem((3, nz)),
            sem((3, 2 * nz)),
            sem((3, n)),
            sem((n,)),
            sem((n,)),
            sem((nh,)),
            sem((nz,)),
            sem((nh,)),
            sem((n - 1,)),
            sem((n,)),
            sem((nh,)),
            sem((nh,)),
            sem((4,)),
            sem((4,)),
        ],
        compiler_params=pltpu.CompilerParams(
            collective_id=0, has_side_effects=True, vmem_limit_bytes=58 * 1024 * 1024
        ),
    )(
        inputs.T, target.T, enc_weight, enc_bias[None, :], dec_weight, dec_bias[None, :],
        skip_weight.T, block_ids.T,
    )
    return (ge, gd, gs.T)


def local(
    inputs,
    target,
    enc_weight,
    enc_bias,
    dec_weight,
    dec_bias,
    skip_weight,
    block_ids,
    slot_lists,
    slot_counts,
):
    tok_rows, feat_dev = inputs.shape
    feat, lat_dev = enc_weight.shape
    owner = lax.axis_index("dict")
    n_dict = lax.axis_size("dict")
    n_tok = lax.axis_size("tok")
    nz = n_dict // 4
    aligned = tok_rows % 128 == 0 and enc_weight.shape[0] % 256 == 0 and feat_dev % 32 == 0 and lat_dev == 128
    if n_tok == 2 and nz % 2 == 0 and nz * 4 == n_dict and aligned:
        return fused(
            nz, inputs, target, enc_weight, enc_bias, dec_weight, dec_bias, skip_weight, block_ids
        )
    scale = 1.0 / math.sqrt(tok_rows * n_tok)
    f32, bf16 = jnp.float32, jnp.bfloat16
    blocks = (owner * lat_dev + jnp.arange(lat_dev, dtype=jnp.int32)) // BLK
    active = jnp.any(block_ids[:, :, None] == blocks[None, None, :], axis=1)
    whole = lax.all_gather(inputs, "dict")
    dec_cols = lax.all_to_all(
        dec_weight.reshape(lat_dev, n_dict, feat_dev), "dict", split_axis=1, concat_axis=0, tiled=True
    ).reshape(n_dict * lat_dev, feat_dev)
    enc_blocks = enc_weight.reshape(n_dict, feat_dev, lat_dev)
    pre = jnp.einsum("btf,bfl->tl", whole, enc_blocks, preferred_element_type=f32) + enc_bias[None, :]
    value, slope = gelu_pair(pre)
    code = jnp.where(active, value, 0.0).astype(bf16)
    codes = lax.all_gather(code, "dict", axis=1, tiled=True)
    skip = jnp.einsum(
        "btf,bfm->tm", whole, skip_weight.reshape(n_dict, feat_dev, feat_dev), preferred_element_type=f32
    )
    recon = jnp.dot(codes, dec_cols, preferred_element_type=f32)
    err = recon + skip + dec_bias[None, :] - target.astype(f32)
    grad_out = (err * scale).astype(bf16)
    back = lax.dot_general(
        dec_cols, grad_out, (((1,), (1,)), ((), ())), preferred_element_type=f32
    ).astype(bf16)
    back = lax.all_to_all(
        back.reshape(n_dict, lat_dev, tok_rows), "dict", split_axis=0, concat_axis=0
    )
    skip_term = jnp.einsum("btf,tm->bfm", whole, grad_out, preferred_element_type=f32)
    skip_term = skip_term.reshape(feat, feat_dev).astype(bf16)
    grad_skip = lax.psum_scatter(skip_term, "tok", scatter_dimension=0, tiled=True).astype(f32)
    dec_term = lax.dot_general(
        codes, grad_out, (((0,), (0,)), ((), ())), preferred_element_type=f32
    ).astype(bf16)
    dec_term = lax.all_to_all(
        dec_term.reshape(n_dict, lat_dev, feat_dev), "dict", split_axis=0, concat_axis=0
    )
    dec_term = lax.psum_scatter(dec_term, "tok", scatter_dimension=0, tiled=True)
    grad_dec = dec_term.transpose(1, 0, 2).reshape(lat_dev, feat // n_tok).astype(f32)
    total = jnp.sum(back.astype(f32), axis=0).T
    dpre = jnp.where(active, total * slope, 0.0).astype(bf16)
    enc_term = jnp.einsum("btf,tl->bfl", whole, dpre, preferred_element_type=f32)
    enc_term = enc_term.reshape(feat, lat_dev).astype(bf16)
    grad_enc = lax.psum_scatter(enc_term, "tok", scatter_dimension=0, tiled=True).astype(f32)
    return (grad_enc, grad_dec, grad_skip)


def solution(mesh):
    in_specs = (
        P("tok", "dict"),
        P("tok", "dict"),
        P(None, "dict"),
        P("dict"),
        P("dict", None),
        P("dict"),
        P(None, "dict"),
        P("tok", None),
        P("tok", None, None),
        P("tok", None),
    )
    out_specs = (P("tok", "dict"), P("dict", "tok"), P("tok", "dict"))
    return jax.shard_map(local, mesh=mesh, in_specs=in_specs, out_specs=out_specs, check_vma=False)
```

```python
import functools
import math

import jax
import jax.numpy as jnp
from jax import lax
from jax.experimental import pallas as pl
from jax.experimental.pallas import tpu as pltpu
from jax.sharding import PartitionSpec as P

BLK = 16
MESH = pl.DeviceIdType.MESH


def gelu_pair(pre):
    factor = math.sqrt(2.0 / math.pi)
    inner = jnp.tanh(factor * (pre + 0.044715 * pre * pre * pre))
    value = 0.5 * pre * (1.0 + inner)
    slope = 0.5 * (1.0 + inner) + 0.5 * pre * (1.0 - inner * inner) * factor * (
        1.0 + 3.0 * 0.044715 * pre * pre
    )
    return (value, slope)


def dot(a, b, da, db):
    return lax.dot_general(a, b, (((da,), (db,)), ((), ())), preferred_element_type=jnp.float32)


def fused_kernel(
    nz, scale,
    xt, tt, enc, eb, dec, db, sw, ids,
    ge, gd, gs,
    encv, decv, swv, x_all, x_oth, dec_t, dec_cols, codes, go_all, go_oth, gd_part, gd_recv,
    dpre, dpre_oth, skip_acc, pre_acc, slope_s,
    gs_v, load_sem, up_send, down_send, y_send, sib_send, ag_recv, dx_send, dx_recv, xo_send, xo_fwd, xo_recv, dec_send, dec_recv, gd_send, gd_recv_sem,
    pair_send, pair_recv,
):
    f32, bf16 = jnp.float32, jnp.bfloat16
    n = 4 * nz
    nh = n // 2
    t, me = lax.axis_index("tok"), lax.axis_index("dict")
    z, y, c = me // 4, (me // 2) % 2, me % 2
    fd, lat = xt.shape[0], enc.shape[1]
    half = fd // 2

    def at(zz, yy, cc):
        return (zz * 2 + yy) * 2 + cc

    def rows(i, size):
        return pl.ds(pl.multiple_of(i * size, 16), size)

    sib, ypeer = (t, at(z, y, 1 - c)), (t, at(z, 1 - y, c))
    xpeer = (1 - t, me)

    def copy(src, dst, s, r, dev):
        return pltpu.make_async_remote_copy(
            src_ref=src, dst_ref=dst, send_sem=s, recv_sem=r, device_id=dev, device_id_type=MESH
        )

    pending = []

    def send(src, dst, s, r, dev):
        cp = copy(src, dst, s, r, dev)
        cp.start()
        pending.append(cp)

    def arrived(ref, r):
        copy(ref, ref, pair_send.at[0], r, xpeer).wait_recv()

    def step(ref, s, r, dev):
        copy(ref, ref, s, r, dev).start()

    def pass_on(p, buf, size, zb):
        d = at(zb, y, c)
        blk = buf.at[rows(d, size)]
        step(blk, y_send.at[p, zb], ag_recv.at[p, d], ypeer)
        step(blk, sib_send.at[p, zb * 2 + y], ag_recv.at[p, d], sib)

    def chain(p, buf, size, zb, up):
        d = at(zb, y, c)
        blk = buf.at[rows(d, size)]

        @pl.when((z < nz - 1) if up else (z > 0))
        def _():
            to = (t, at(z + 1, y, c) if up else at(z - 1, y, c))
            step(blk, (up_send if up else down_send).at[p, zb], ag_recv.at[p, d], to)

    def gather_own(p, buf, size):
        chain(p, buf, size, z, True)
        chain(p, buf, size, z, False)
        pass_on(p, buf, size, z)

    def at_step(k, use):
        if k == 0:
            use(z, True)
            return
        for up in (True, False):
            zb = z - k if up else z + k

            @pl.when((zb >= 0) if up else (zb < nz))
            def _():
                use(zb, up)

    def gather(p, buf, size, extra, consume, between=lambda k: None):
        def from_z(zb, up):
            d = at(zb, y, c)
            arrived(buf.at[rows(d, size)], ag_recv.at[p, d])
            chain(p, buf, size, zb, up)
            pass_on(p, buf, size, zb)
            extra(d, zb)

        def from_y(zb, up):
            d = at(zb, 1 - y, c)
            blk = buf.at[rows(d, size)]
            arrived(blk, ag_recv.at[p, d])
            step(blk, sib_send.at[p, zb * 2 + 1 - y], ag_recv.at[p, d], sib)
            extra(d, zb)

        def near(zb, up):
            consume(at(zb, y, c))
            other = at(zb, y, 1 - c)
            arrived(buf.at[rows(other, size)], ag_recv.at[p, other])
            consume(other)

        def far(zb, up):
            consume(at(zb, 1 - y, c))
            other = at(zb, 1 - y, 1 - c)
            arrived(buf.at[rows(other, size)], ag_recv.at[p, other])
            consume(other)

        extra(me, z)
        for k in range(1, nz + 2):
            if k < nz:
                at_step(k, from_z)
            if k <= nz:
                at_step(k - 1, from_y)
            between(k)
            if k <= nz:
                at_step(k - 1, near)
            if k > 1:
                at_step(k - 2, far)

    def drain(p, buf, size):
        blk = buf.at[rows(me, size)]

        def sent(s):
            copy(blk, blk, s, ag_recv.at[p, me], sib).wait_send()

        for zb in range(nz):
            sent(y_send.at[p, zb])
            sent(sib_send.at[p, zb * 2])
            sent(sib_send.at[p, zb * 2 + 1])
            if zb < nz - 1:
                @pl.when((zb <= z) & (z < nz - 1))
                def _():
                    sent(up_send.at[p, zb])
            if zb > 0:
                @pl.when((zb >= z) & (z > 0))
                def _():
                    sent(down_send.at[p, zb])

    def nothing(d, zz):
        pass

    barrier = pltpu.get_barrier_semaphore()
    pl.semaphore_signal(barrier, inc=1, device_id=xpeer, device_id_type=MESH)
    for k in range(1, n):
        pl.semaphore_signal(barrier, inc=1, device_id=(t, (me + k) % n), device_id_type=MESH)
    loads = [
        pltpu.make_async_copy(s, d, load_sem.at[i])
        for i, (s, d) in enumerate(((dec, decv), (enc, encv), (sw, swv)))
    ]
    for cp in loads:
        cp.start()
    x_all[rows(me, fd), :] = xt[...]
    pre_acc[...] = jnp.zeros_like(pre_acc)
    pl.semaphore_wait(barrier, n)

    gather_own(0, x_all, fd)
    loads[0].wait()
    width = dec_t.shape[1]
    for j in range(dec_t.shape[0] // width):
        dec_t[j * width : (j + 1) * width, :] = decv[:, j * width : (j + 1) * width].T

    def to_other(d, zz):
        @pl.when(zz // (nz // 2) == 1 - t)
        def _():
            j = d % nh
            copy(
                x_all.at[rows(d, fd)], x_oth.at[rows(j, fd)], xo_send.at[j], xo_recv.at[j], xpeer
            ).start()

    cols = pl.ds(pl.multiple_of(me * lat, 128), lat)
    part = pl.ds(pl.multiple_of(t * half, 16), half)

    def dec_columns(k):
        if k != max(1, nz - 1):
            return
        for i in range(1, n):
            d = (me + i) % n
            send(
                dec_t.at[pl.ds(pl.multiple_of(d * fd + t * half, 16), half)],
                dec_cols.at[part, cols],
                dec_send.at[i - 1],
                dec_recv.at[me],
                (t, d),
            )
        dec_cols[part, cols] = dec_t[pl.ds(pl.multiple_of(me * fd + t * half, 16), half), :]

    loads[1].wait()

    def consume(d):
        r = rows(d, fd)
        blk = x_all[r, :]
        pre_acc[...] += dot(encv[r, :], blk, 0, 0)

    gather(0, x_all, fd, to_other, consume, dec_columns)

    def column(row):
        size = row.shape[1]
        eye = lax.broadcasted_iota(jnp.int32, (size, size), 0) == lax.broadcasted_iota(
            jnp.int32, (size, size), 1
        )
        return jnp.sum(jnp.where(eye, row, 0.0), axis=1, keepdims=True)

    pre = pre_acc[...] + column(eb[...])
    value, slope = gelu_pair(pre)
    blocks = lax.broadcasted_iota(jnp.int32, pre.shape, 0) // BLK + me * (lat // BLK)
    active = ids[0:1, :] == blocks
    for r in range(1, ids.shape[0]):
        active = active | (ids[r : r + 1, :] == blocks)
    slope_s[...] = jnp.where(active, slope, 0.0)
    code = jnp.where(active, value, 0.0).astype(bf16)
    codes[rows(me, lat), :] = code

    gather_own(1, codes, lat)
    loads[2].wait()
    wide = 512 if swv.shape[1] % 512 == 0 else 128
    skip_acc[...] = column(db[...]) - tt[...].astype(f32)

    def skip_cols(j, carry):
        r = pl.ds(pl.multiple_of(j * wide, 128), wide)
        skip_acc[...] += dot(swv[:, r], x_all[r, :], 1, 0)
        return carry

    lax.fori_loop(0, swv.shape[1] // wide, skip_cols, 0)

    def dec_to_other(k):
        if k == 1:
            for i in range(n):
                d = (me + i) % n
                blk = dec_cols.at[part, pl.ds(pl.multiple_of(d * lat, 128), lat)]
                if i:
                    arrived(blk, dec_recv.at[d])
                send(blk, blk, dx_send.at[i], dx_recv.at[d], xpeer)

    gather(1, codes, lat, nothing, lambda d: None, dec_to_other)
    other = pl.ds(pl.multiple_of((1 - t) * half, 16), half)
    for d in range(n):
        arrived(dec_cols.at[other, d * lat : (d + 1) * lat], dx_recv.at[d])
    err = dot(dec_cols[...], codes[...], 1, 0) + skip_acc[...]
    go = (err * scale).astype(bf16)
    go_all[rows(me, fd), :] = go
    pre_acc[...] = jnp.zeros_like(pre_acc)

    own_go = go_all.at[rows(me, fd)]
    gather_own(2, go_all, fd)
    send(own_go, go_oth, pair_send.at[2], pair_recv.at[2], xpeer)
    for zl in range(nz // 2):
        for yy in range(2):
            j = at(zl, yy, c)
            blk = x_oth.at[rows(j, fd)]
            arrived(blk, xo_recv.at[j])
            send(blk, blk, xo_fwd.at[zl * 2 + yy], xo_recv.at[j], sib)
    tall = 256 if gs_v.shape[1] % 256 == 0 else 128
    gs_copy = pltpu.make_async_copy(gs_v, gs, load_sem.at[3])

    def grad_skip(k):
        if k == max(1, nz - 2):
            for zl in range(nz // 2):
                for yy in range(2):
                    j = at(zl, yy, 1 - c)
                    arrived(x_oth.at[rows(j, fd)], xo_recv.at[j])
            arrived(go_oth, pair_recv.at[2])

            def body(j, carry):
                r = pl.ds(pl.multiple_of(j * tall, 128), tall)
                mine = x_all[pl.ds(pl.multiple_of(t * nh * fd + j * tall, 16), tall), :]
                gs_v[:, r] = dot(go_all[rows(me, fd), :], mine, 1, 1) + dot(
                    go_oth[...], x_oth[r, :], 1, 1
                )
                return carry

            lax.fori_loop(0, gs_v.shape[1] // tall, body, 0)
            gs_copy.start()

    def back(d):
        r = rows(d, fd)
        blk = go_all[r, :]
        pre_acc[...] += dot(dec_t[r, :], blk, 0, 0)
        gd_part[r, :] = dot(blk, codes[rows(me, lat), :], 1, 1).astype(bf16)

        @pl.when(d // nh == 1 - t)
        def _():
            j = d % nh
            copy(
                gd_part.at[r], gd_recv.at[rows(j, fd)], gd_send.at[j], gd_recv_sem.at[j], xpeer
            ).start()

    gather(2, go_all, fd, nothing, back, grad_skip)
    dpre[...] = (pre_acc[...] * slope_s[...]).astype(bf16)
    send(dpre, dpre_oth, pair_send.at[3], pair_recv.at[3], xpeer)


    for j in range(nh):
        arrived(gd_recv.at[rows(j, fd)], gd_recv_sem.at[j])

    def dec_rows(j, carry):
        r = rows(j, lat)
        mine = gd_part[pl.ds(pl.multiple_of(t * nh * fd + j * lat, 16), lat), :]
        total = mine.astype(f32) + gd_recv[r, :].astype(f32)
        gd[:, pl.ds(pl.multiple_of(j * lat, 128), lat)] = total.T
        return carry

    lax.fori_loop(0, nh * fd // lat, dec_rows, 0)
    arrived(dpre_oth, pair_recv.at[3])

    def enc_rows(j, carry):
        r = rows(j, fd)
        mine = x_all[rows(t * nh + j, fd), :]
        ge[r, :] = dot(mine, dpre[...], 1, 1) + dot(x_oth[r, :], dpre_oth[...], 1, 1)
        return carry

    lax.fori_loop(0, nh, enc_rows, 0)
    gs_copy.wait()
    drain(0, x_all, fd)
    drain(1, codes, lat)
    drain(2, go_all, fd)
    for cp in pending:
        cp.wait_send()
    for zl in range(nz // 2):
        for yy in range(2):
            j = at(zl, yy, c)
            blk = x_oth.at[rows(j, fd)]
            copy(blk, blk, xo_send.at[j], xo_recv.at[j], xpeer).wait_send()
    for j in range(nh):
        blk = gd_recv.at[rows(j, fd)]
        copy(blk, blk, gd_send.at[j], gd_recv_sem.at[j], xpeer).wait_send()


def fused(nz, inputs, target, enc_weight, enc_bias, dec_weight, dec_bias, skip_weight, block_ids):
    tok, fd = inputs.shape
    feat, lat = enc_weight.shape
    n = 4 * nz
    nh = n // 2
    f32, bf16 = jnp.float32, jnp.bfloat16
    vm, hbm = pl.BlockSpec(memory_space=pltpu.VMEM), pl.BlockSpec(memory_space=pl.ANY)
    sem = pltpu.SemaphoreType.DMA
    ge, gd, gs = pl.pallas_call(
        functools.partial(fused_kernel, nz, 1.0 / math.sqrt(2 * tok)),
        out_shape=(
            jax.ShapeDtypeStruct((feat // 2, lat), f32),
            jax.ShapeDtypeStruct((lat, feat // 2), f32),
            jax.ShapeDtypeStruct((fd, feat // 2), f32),
        ),
        in_specs=[vm, vm, hbm, vm, hbm, vm, hbm, vm],
        out_specs=(vm, vm, hbm),
        scratch_shapes=[
            pltpu.VMEM((feat, lat), bf16),
            pltpu.VMEM((lat, feat), bf16),
            pltpu.VMEM((fd, feat), bf16),
            pltpu.VMEM((feat, tok), bf16),
            pltpu.VMEM((feat // 2, tok), bf16),
            pltpu.VMEM((feat, lat), bf16),
            pltpu.VMEM((fd, n * lat), bf16),
            pltpu.VMEM((n * lat, tok), bf16),
            pltpu.VMEM((feat, tok), bf16),
            pltpu.VMEM((fd, tok), bf16),
            pltpu.VMEM((feat, lat), bf16),
            pltpu.VMEM((feat // 2, lat), bf16),
            pltpu.VMEM((lat, tok), bf16),
            pltpu.VMEM((lat, tok), bf16),
            pltpu.VMEM((fd, tok), f32),
            pltpu.VMEM((lat, tok), f32),
            pltpu.VMEM((lat, tok), f32),
            pltpu.VMEM((fd, feat // 2), f32),
            sem((4,)),
            sem((3, nz)),
            sem((3, nz)),
            sem((3, nz)),
            sem((3, 2 * nz)),
            sem((3, n)),
            sem((n,)),
            sem((n,)),
            sem((nh,)),
            sem((nz,)),
            sem((nh,)),
            sem((n - 1,)),
            sem((n,)),
            sem((nh,)),
            sem((nh,)),
            sem((4,)),
            sem((4,)),
        ],
        compiler_params=pltpu.CompilerParams(
            collective_id=0, has_side_effects=True, vmem_limit_bytes=58 * 1024 * 1024
        ),
    )(
        inputs.T, target.T, enc_weight, enc_bias[None, :], dec_weight, dec_bias[None, :],
        skip_weight.T, block_ids.T,
    )
    return (ge, gd, gs.T)


def local(
    inputs,
    target,
    enc_weight,
    enc_bias,
    dec_weight,
    dec_bias,
    skip_weight,
    block_ids,
    slot_lists,
    slot_counts,
):
    tok_rows, feat_dev = inputs.shape
    feat, lat_dev = enc_weight.shape
    owner = lax.axis_index("dict")
    n_dict = lax.axis_size("dict")
    n_tok = lax.axis_size("tok")
    nz = n_dict // 4
    aligned = tok_rows % 128 == 0 and enc_weight.shape[0] % 256 == 0 and feat_dev % 32 == 0 and lat_dev == 128
    if n_tok == 2 and nz % 2 == 0 and nz * 4 == n_dict and aligned:
        return fused(
            nz, inputs, target, enc_weight, enc_bias, dec_weight, dec_bias, skip_weight, block_ids
        )
    scale = 1.0 / math.sqrt(tok_rows * n_tok)
    f32, bf16 = jnp.float32, jnp.bfloat16
    blocks = (owner * lat_dev + jnp.arange(lat_dev, dtype=jnp.int32)) // BLK
    active = jnp.any(block_ids[:, :, None] == blocks[None, None, :], axis=1)
    whole = lax.all_gather(inputs, "dict")
    dec_cols = lax.all_to_all(
        dec_weight.reshape(lat_dev, n_dict, feat_dev), "dict", split_axis=1, concat_axis=0, tiled=True
    ).reshape(n_dict * lat_dev, feat_dev)
    enc_blocks = enc_weight.reshape(n_dict, feat_dev, lat_dev)
    pre = jnp.einsum("btf,bfl->tl", whole, enc_blocks, preferred_element_type=f32) + enc_bias[None, :]
    value, slope = gelu_pair(pre)
    code = jnp.where(active, value, 0.0).astype(bf16)
    codes = lax.all_gather(code, "dict", axis=1, tiled=True)
    skip = jnp.einsum(
        "btf,bfm->tm", whole, skip_weight.reshape(n_dict, feat_dev, feat_dev), preferred_element_type=f32
    )
    recon = jnp.dot(codes, dec_cols, preferred_element_type=f32)
    err = recon + skip + dec_bias[None, :] - target.astype(f32)
    grad_out = (err * scale).astype(bf16)
    back = lax.dot_general(
        dec_cols, grad_out, (((1,), (1,)), ((), ())), preferred_element_type=f32
    ).astype(bf16)
    back = lax.all_to_all(
        back.reshape(n_dict, lat_dev, tok_rows), "dict", split_axis=0, concat_axis=0
    )
    skip_term = jnp.einsum("btf,tm->bfm", whole, grad_out, preferred_element_type=f32)
    skip_term = skip_term.reshape(feat, feat_dev).astype(bf16)
    grad_skip = lax.psum_scatter(skip_term, "tok", scatter_dimension=0, tiled=True).astype(f32)
    dec_term = lax.dot_general(
        codes, grad_out, (((0,), (0,)), ((), ())), preferred_element_type=f32
    ).astype(bf16)
    dec_term = lax.all_to_all(
        dec_term.reshape(n_dict, lat_dev, feat_dev), "dict", split_axis=0, concat_axis=0
    )
    dec_term = lax.psum_scatter(dec_term, "tok", scatter_dimension=0, tiled=True)
    grad_dec = dec_term.transpose(1, 0, 2).reshape(lat_dev, feat // n_tok).astype(f32)
    total = jnp.sum(back.astype(f32), axis=0).T
    dpre = jnp.where(active, total * slope, 0.0).astype(bf16)
    enc_term = jnp.einsum("btf,tl->bfl", whole, dpre, preferred_element_type=f32)
    enc_term = enc_term.reshape(feat, lat_dev).astype(bf16)
    grad_enc = lax.psum_scatter(enc_term, "tok", scatter_dimension=0, tiled=True).astype(f32)
    return (grad_enc, grad_dec, grad_skip)


def solution(mesh):
    in_specs = (
        P("tok", "dict"),
        P("tok", "dict"),
        P(None, "dict"),
        P("dict"),
        P("dict", None),
        P("dict"),
        P(None, "dict"),
        P("tok", None),
        P("tok", None, None),
        P("tok", None),
    )
    out_specs = (P("tok", "dict"), P("dict", "tok"), P("tok", "dict"))
    return jax.shard_map(local, mesh=mesh, in_specs=in_specs, out_specs=out_specs, check_vma=False)
```
